512 devices in a mesh: dp: 16 (over y_lo, x, core), field: 32 (over y_hi, z).
Axes of the slice: x: 4, y: 4 (y_hi: 2, y_lo: 2; y = y_hi * 2 + y_lo), z: 16, core: 2. Of those that a mesh axis runs over, the one named last changes fastest.
Arguments:
- vectors: bfloat16 [16384, 32, 32, 16], P('dp', 'field'), may hold values from -6 to 6
- labels: int32 [16384], P('dp'), may hold values 0 or 1
- pair_weight: bfloat16 [32, 32, 16, 400], P('field'), may hold values from -0.046875 to 0.046875
- hidden_bias: float32 [400], replicated, may hold values from -3 to 3
- mid_weight: bfloat16 [400, 400], replicated, may hold values from -0.3125 to 0.3125
- mid_bias: float32 [400], replicated, may hold values from -3 to 3
- out_weight: float32 [400], replicated, may hold values from -1.5 to 1.5
Outputs:
- vector_grad: bfloat16 [16384, 32, 32, 16], P('dp', 'field')
- grad_pair: float32 [32, 32, 16, 400], P('field')
- grad_hidden_bias: float32 [400], replicated
- grad_mid: float32 [400, 400], replicated
- grad_mid_bias: float32 [400], replicated
- grad_out: float32 [400], replicated
The draws below stay inside these ranges and needn't reach their ends.
All inputs are finite; a program needn't handle non-finite values. No bound on the sum of `labels` on one device may be relied on, other than what follows from the above.
Results may differ from the reference program's by a relative error of at most 0.0074.
Values may be sent and summed in bfloat16 or wider, within the bound.
A program may use at most 64 MiB of HBM per device.

```python
import jax
import jax.numpy as jnp
from jax import lax

FIELDS = 32
DIM = 16
HIDDEN_SIZE = 400
GROUP_ROWS = 1024
BATCH = 16384
N_DP = 16


def touch_ends(values, own_key, low, top_value):
    place = [jax.random.randint(jax.random.fold_in(own_key, axis), (), 0, length) for axis, length in enumerate(values.shape)]
    main_axis = values.shape.index(max(values.shape))
    neighbour = place[:main_axis] + [(place[main_axis] + 1) % values.shape[main_axis]] + place[main_axis + 1:]
    return values.at[tuple(place)].set(low).at[tuple(neighbour)].set(top_value)


def block_scale(stream_key, extent, pieces, low, high):
    def one(dim, parts):
        heights = jax.random.uniform(jax.random.fold_in(jax.random.fold_in(stream_key, 6), dim), (parts,), jnp.float32, low / len(pieces), high / len(pieces))
        return jnp.repeat(jnp.exp(heights), extent[dim] // parts).reshape((-1,) + (1,) * (len(extent) - dim - 1))

    loudness = one(*pieces[0])
    for cut in pieces[1:]:
        loudness = loudness * one(*cut)
    return loudness


def centred(own_key, dims, width, limit, cuts=(), held_as=jnp.bfloat16):
    factor_of = block_scale(own_key, dims, cuts, -0.22, 0.18) if cuts else 1.0
    entries = jax.random.normal(own_key, dims, jnp.float32) * width * factor_of
    return jnp.minimum(jnp.maximum(entries, -limit), limit).astype(held_as)


def setup_inputs(seed: int = 0) -> dict:
    arg_keys = jax.random.split(jax.random.key(seed), 8)
    return {
        "vectors": centred(arg_keys[0], (BATCH, FIELDS, FIELDS, DIM), 1.0, 6.0, ((0, 16), (1, 32))),
        "labels": touch_ends((jax.random.randint(arg_keys[1], (BATCH,), 0, 4) < 1).astype(jnp.int32), jax.random.fold_in(arg_keys[1], 1), 0, 1),
        "pair_weight": centred(arg_keys[2], (FIELDS, FIELDS, DIM, HIDDEN_SIZE), (FIELDS * (FIELDS - 1) * DIM) ** -0.5, 0.046875, ((0, 32),)),
        "hidden_bias": centred(arg_keys[3], (HIDDEN_SIZE,), 0.5, 3.0, (), jnp.float32),
        "mid_weight": centred(arg_keys[4], (HIDDEN_SIZE, HIDDEN_SIZE), HIDDEN_SIZE ** -0.5, 0.3125),
        "mid_bias": centred(arg_keys[5], (HIDDEN_SIZE,), 0.5, 3.0, (), jnp.float32),
        "out_weight": centred(arg_keys[6], (HIDDEN_SIZE,), 0.25, 1.5, (), jnp.float32),
    }


def silu_parts(preact):
    squash = jax.nn.sigmoid(preact)
    return preact * squash, squash * (1.0 + preact * (1.0 - squash))


def contract_rows(left, right):
    return lax.dot_general(left, right, (((0,), (0,)), ((), ())), preferred_element_type=jnp.float32)


def reference(vectors, labels, pair_weight, hidden_bias, mid_weight, mid_bias, out_weight):
    keep_mask = (1.0 - jnp.eye(FIELDS, dtype=jnp.float32))[:, :, None]
    weight_flat = pair_weight.reshape(FIELDS * FIELDS * DIM, HIDDEN_SIZE)
    stacked = vectors.reshape(N_DP, GROUP_ROWS, FIELDS, FIELDS, DIM)
    stacked_labels = labels.reshape(N_DP, GROUP_ROWS)

    def one_group(totals, inputs):
        group_vectors, group_labels = inputs
        direct = group_vectors.astype(jnp.float32)
        partner = jnp.swapaxes(direct, 1, 2)
        pair_feats = (direct * partner * keep_mask).astype(jnp.bfloat16).reshape(GROUP_ROWS, FIELDS * FIELDS * DIM)
        hidden_pre = jnp.dot(pair_feats, weight_flat, preferred_element_type=jnp.float32) + hidden_bias
        hidden_full, hidden_slope = silu_parts(hidden_pre)
        hidden_act = hidden_full.astype(jnp.bfloat16)
        mid_pre = jnp.dot(hidden_act, mid_weight, preferred_element_type=jnp.float32) + mid_bias
        mid_act, mid_slope = silu_parts(mid_pre)
        logit = jnp.sum(mid_act * out_weight, axis=1)
        logit_grad = jax.nn.sigmoid(logit) - group_labels.astype(jnp.float32)
        out_term = jnp.sum(logit_grad[:, None] * mid_act, axis=0)
        mid_grad = (logit_grad[:, None] * out_weight * mid_slope).astype(jnp.bfloat16)
        mid_term = contract_rows(hidden_act, mid_grad)
        mid_bias_term = jnp.sum(mid_grad.astype(jnp.float32), axis=0)
        hidden_back = jnp.dot(mid_grad, mid_weight.T, preferred_element_type=jnp.float32)
        hidden_grad = (hidden_back * hidden_slope).astype(jnp.bfloat16)
        hidden_bias_term = jnp.sum(hidden_grad.astype(jnp.float32), axis=0)
        pair_term = contract_rows(pair_feats, hidden_grad)
        pair_grad = lax.dot_general(hidden_grad, weight_flat, (((1,), (1,)), ((), ())), preferred_element_type=jnp.float32)
        pair_grad = pair_grad.reshape(GROUP_ROWS, FIELDS, FIELDS, DIM) * keep_mask
        group_grad = ((pair_grad + jnp.swapaxes(pair_grad, 1, 2)) * partner).astype(jnp.bfloat16)
        updated = (totals[0] + pair_term, totals[1] + hidden_bias_term, totals[2] + mid_term,
                   totals[3] + mid_bias_term, totals[4] + out_term)
        return updated, group_grad

    start = (jnp.zeros((FIELDS * FIELDS * DIM, HIDDEN_SIZE), jnp.float32), jnp.zeros((HIDDEN_SIZE,), jnp.float32),
             jnp.zeros((HIDDEN_SIZE, HIDDEN_SIZE), jnp.float32), jnp.zeros((HIDDEN_SIZE,), jnp.float32),
             jnp.zeros((HIDDEN_SIZE,), jnp.float32))
    totals, grads = lax.scan(one_group, start, (stacked, stacked_labels))
    vector_grad = grads.reshape(BATCH, FIELDS, FIELDS, DIM)
    grad_pair = totals[0].reshape(FIELDS, FIELDS, DIM, HIDDEN_SIZE)
    return vector_grad, grad_pair, totals[1], totals[2], totals[3], totals[4]
```

```python
import functools

import jax
import jax.numpy as jnp
from jax import lax
from jax.experimental import pallas as pl
from jax.experimental.pallas import tpu as pltpu
from jax.sharding import PartitionSpec as P

F32 = jnp.float32
BF16 = jnp.bfloat16
MESH = pl.DeviceIdType.MESH


def silu_parts(v):
    s = jax.nn.sigmoid(v)
    return v * s, s * (1.0 + v * (1.0 - s))


def drain(ref, sem):
    pltpu.make_async_copy(ref, ref, sem).wait()


def kernel(
    n_dp, n_f, dim, act_ranks,
    v_ref, lab_ref, w_ref, hb_ref, mw_ref, mb_ref, ow_ref,
    vg_ref, gp_ref, gm_ref,
    p_ref, feat_ref, wt_ref, part_ref, first_ref, up_ref, dn_ref, yx_ref,
    hg_ref, gmt_ref, gmr_ref, z1_ref, z2_ref, y2_ref, gmf_ref,
    gpt_ref, gpr_ref, gpf_ref,
    one, rs_up, rs_dn, ag_up, ag_dn,
):
    (a2a_s, a2a_r, w_s, w_r, wg_s, wg_r, up_s, dn_s, yx_s, yx_r, agu_s, agd_s, agy_s, agy_r,
     gm_s, gm_r, z1_s, z1_r, z2_s, z2_r, y2_s, y2_r, gmg_s, gmg_r, gp_s, gp_r, gpg_s, gpg_r) = [
        one.at[i] for i in range(28)]
    n_z = n_f // 2
    hops_up, hops_dn = n_z // 2, n_z // 2 - 1
    d, f = lax.axis_index("dp"), lax.axis_index("field")
    yh, z = f // n_z, f % n_z
    f_up = yh * n_z + (z + 1) % n_z
    f_dn = yh * n_z + (z + n_z - 1) % n_z
    f_y = (1 - yh) * n_z + z
    share = part_ref.shape[1]
    units = w_ref.shape[1]
    per = n_f // n_dp

    def send(src, dst, s, r, to_d, to_f):
        pltpu.make_async_remote_copy(
            src_ref=src, dst_ref=dst, send_sem=s, recv_sem=r,
            device_id=(to_d, to_f), device_id_type=MESH,
        ).start()

    def rows(i, n):
        return pl.ds(pl.multiple_of(i * n, n), n)

    barrier = pltpu.get_barrier_semaphore()

    def greet_f(o, _):
        pl.semaphore_signal(barrier, inc=1, device_id=(d, (f + o) % n_f), device_id_type=MESH)
        return 0

    def greet_d(o, _):
        pl.semaphore_signal(barrier, inc=1, device_id=((d + o) % n_dp, f), device_id_type=MESH)
        return 0

    lax.fori_loop(1, n_f, greet_f, 0)
    lax.fori_loop(1, n_dp, greet_d, 0)
    pl.semaphore_wait(barrier, n_f + n_dp - 2)

    @pl.when(d == f // per)
    def _():
        def body(o, _):
            j = (f + o) % n_f
            send(w_ref.at[rows(j, dim)], wt_ref.at[rows(f, dim)], w_s, w_r, d, j)
            return 0
        lax.fori_loop(1, n_f, body, 0)
        wt_ref[rows(f, dim), :] = w_ref[rows(f, dim), :]

    def a2a(o, _):
        j = (f + o) % n_f
        send(v_ref.at[rows(j, dim)], p_ref.at[rows(f, dim)], a2a_s, a2a_r, d, j)
        return 0

    lax.fori_loop(1, n_f, a2a, 0)
    p_ref[rows(f, dim), :] = jnp.zeros((dim, p_ref.shape[1]), BF16)

    @pl.when(d == f // per)
    def _():
        drain(wt_ref.at[pl.ds(0, dim * (per - 1))], w_r)

    @pl.when(d != f // per)
    def _():
        drain(wt_ref.at[pl.ds(0, dim * per)], w_r)

    def pass_on(o, _):
        block = wt_ref.at[rows(d, dim * per)]
        send(block, block, wg_s, wg_r, (d + o) % n_dp, f)
        return 0

    lax.fori_loop(1, n_dp, pass_on, 0)

    drain(p_ref.at[pl.ds(0, dim * (n_f - 1))], a2a_r)

    n_ex = v_ref.shape[1]
    step = min(256, n_ex)
    for c in range(n_ex // step):
        cols = pl.ds(c * step, step)
        feats = (v_ref[:, cols].astype(F32) * p_ref[:, cols].astype(F32)).astype(BF16)
        feat_ref[:, cols] = feats
        res = lax.dot_general(feats, w_ref[...], (((0,), (0,)), ((), ())), preferred_element_type=F32)
        part_ref[pl.ds(c * step // share, step // share)] = res.reshape(step // share, share, units)

    def own(y, zz):
        return part_ref[y * n_z + (zz + 2 * n_z) % n_z]

    for y in range(2):
        first_ref[0, y] = own(y, z + hops_up).astype(BF16)
        send(first_ref.at[0, y], up_ref.at[y, 0], up_s, rs_up.at[y, 0], d, f_up)
        first_ref[1, y] = own(y, z - hops_dn).astype(BF16)
        send(first_ref.at[1, y], dn_ref.at[y, 0], dn_s, rs_dn.at[y, 0], d, f_dn)

    def rs_hop(s, with_dn):
        for y in range(2):
            drain(up_ref.at[y, s - 1], rs_up.at[y, s - 1])
            up_ref[y, s - 1] = (up_ref[y, s - 1].astype(F32) + own(y, z + hops_up - s)).astype(BF16)
            send(up_ref.at[y, s - 1], up_ref.at[y, s], up_s, rs_up.at[y, s], d, f_up)
            if with_dn:
                drain(dn_ref.at[y, s - 1], rs_dn.at[y, s - 1])
                dn_ref[y, s - 1] = (dn_ref[y, s - 1].astype(F32) + own(y, z - hops_dn + s)).astype(BF16)
                send(dn_ref.at[y, s - 1], dn_ref.at[y, s], dn_s, rs_dn.at[y, s], d, f_dn)

    def rs_body(s, _):
        rs_hop(s, True)
        return 0

    lax.fori_loop(1, hops_dn, rs_body, 0)
    rs_hop(hops_dn, False)

    for y in range(2):
        drain(dn_ref.at[y, hops_dn - 1], rs_dn.at[y, hops_dn - 1])
        drain(up_ref.at[y, hops_up - 1], rs_up.at[y, hops_up - 1])

    def total(y):
        return (part_ref[y * n_z + z] + up_ref[y, hops_up - 1].astype(F32)) + dn_ref[y, hops_dn - 1].astype(F32)

    yx_ref[0] = total(1 - yh).astype(BF16)
    send(yx_ref.at[0], yx_ref.at[1], yx_s, yx_r, d, f_y)
    mine = total(yh)
    drain(yx_ref.at[1], yx_r)
    pre = mine + yx_ref[1].astype(F32) + hb_ref[...]

    full, slope = silu_parts(pre)
    act = full.astype(BF16)
    mid_pre = jnp.dot(act, mw_ref[...], preferred_element_type=F32) + mb_ref[...]
    mid_act, mid_slope = silu_parts(mid_pre)
    logit = jnp.sum(mid_act * ow_ref[...], axis=1, keepdims=True)
    per_row = 128 // share
    lab = lab_ref[pl.ds(f // per_row, 1), :].astype(F32)
    lane = lax.broadcasted_iota(jnp.int32, (share, 128), 1)
    line = lax.broadcasted_iota(jnp.int32, (share, 128), 0)
    lab = jnp.sum(jnp.where(lane == (f % per_row) * share + line, lab, 0.0), axis=1, keepdims=True)
    lg = jax.nn.sigmoid(logit) - lab
    out_sum = jnp.sum(lg * mid_act, axis=0, keepdims=True)
    mg = (lg * ow_ref[...] * mid_slope).astype(BF16)
    back = lax.dot_general(mg, mw_ref[...], (((1,), (1,)), ((), ())), preferred_element_type=F32)
    hg = (back * slope).astype(BF16)
    hg_ref[f] = hg

    send(hg_ref.at[f], hg_ref.at[f], agy_s, agy_r, d, f_y)
    send(hg_ref.at[f], hg_ref.at[f], agu_s, ag_up.at[0, 0], d, f_up)
    send(hg_ref.at[f], hg_ref.at[f], agd_s, ag_dn.at[0, 0], d, f_dn)

    mid_sum = jnp.sum(mg.astype(F32), axis=0, keepdims=True)
    hid_sum = jnp.sum(hg.astype(F32), axis=0, keepdims=True)
    gmt_ref[pl.ds(0, units), :] = lax.dot_general(
        act, mg, (((0,), (0,)), ((), ())), preferred_element_type=F32).astype(BF16)
    extra = gmt_ref.shape[0] - units
    at = lax.broadcasted_iota(jnp.int32, (extra, units), 0)
    tail = jnp.where(at == 0, mid_sum, jnp.where(at == 1, out_sum, jnp.where(at == 2, hid_sum, 0.0)))
    gmt_ref[pl.ds(units, extra), :] = tail.astype(BF16)
    gm_rows = gmr_ref.shape[1]

    def gm_scatter(o, _):
        to = (d + o) % n_dp

        @pl.when(to < act_ranks)
        def _():
            send(gmt_ref.at[rows(to, gm_rows)], gmr_ref.at[d], gm_s, gm_r, to, f)
        return 0

    lax.fori_loop(1, n_dp, gm_scatter, 0)

    other = (1 - yh) * n_z + z
    drain(hg_ref.at[other], agy_r)
    send(hg_ref.at[other], hg_ref.at[other], agu_s, ag_up.at[1, 0], d, f_up)
    send(hg_ref.at[other], hg_ref.at[other], agd_s, ag_dn.at[1, 0], d, f_dn)

    def ag_hop(t, with_dn):
        for k in range(2):
            base = (yh if k == 0 else 1 - yh) * n_z
            blk = hg_ref.at[base + (z - t + n_z) % n_z]
            drain(blk, ag_up.at[k, t - 1])
            send(blk, blk, agu_s, ag_up.at[k, t], d, f_up)
            blk = hg_ref.at[base + (z + t) % n_z]
            drain(blk, ag_dn.at[k, t - 1])
            if with_dn:
                send(blk, blk, agd_s, ag_dn.at[k, t], d, f_dn)

    def ag_body(t, _):
        ag_hop(t, True)
        return 0

    lax.fori_loop(1, hops_dn, ag_body, 0)
    ag_hop(hops_dn, False)
    for k in range(2):
        base = (yh if k == 0 else 1 - yh) * n_z
        drain(hg_ref.at[base + (z + n_z - hops_up) % n_z], ag_up.at[k, hops_up - 1])

    hg_all = hg_ref[...].reshape(n_ex, units)
    gpt_ref[...] = jnp.dot(feat_ref[...], hg_all, preferred_element_type=F32).astype(BF16)
    gp_rows = gpr_ref.shape[1]

    def gp_scatter(o, _):
        to = (d + o) % n_dp
        send(gpt_ref.at[rows(to, gp_rows)], gpr_ref.at[d], gp_s, gp_r, to, f)
        return 0

    lax.fori_loop(1, n_dp, gp_scatter, 0)
    gpr_ref[d] = gpt_ref[rows(d, gp_rows), :]

    def add_up(ref):
        acc = ref[0].astype(F32)
        for i in range(1, ref.shape[0]):
            acc = acc + ref[i].astype(F32)
        return acc.astype(BF16)

    n_b = z1_ref.shape[0]
    n_a = z2_ref.shape[0]
    za, zb = z // n_b, z % n_b

    @pl.when(d < act_ranks)
    def _():
        gmr_ref[d] = gmt_ref[rows(d, gm_rows), :]
        drain(gmr_ref.at[pl.ds(0, n_dp - 1)], gm_r)
        z1_ref[zb] = add_up(gmr_ref)
        for o in range(1, n_b):
            to = yh * n_z + za * n_b + (zb + o) % n_b
            send(z1_ref.at[zb], z1_ref.at[zb], z1_s, z1_r, d, to)

    drain(wt_ref.at[pl.ds(0, dim * (n_f - per))], wg_r)
    nt = (((1,), (1,)), ((), ()))
    blocks = 4

    def vg_block(i):
        size = v_ref.shape[0] // blocks
        at = pl.ds(i * size, size)
        both = lax.dot_general(w_ref[at, :], hg_all, nt, preferred_element_type=F32)
        both = both + lax.dot_general(wt_ref[at, :], hg_all, nt, preferred_element_type=F32)
        vg_ref[at, :] = (both * p_ref[at, :].astype(F32)).astype(BF16)

    for i in range(2):
        vg_block(i)

    @pl.when(d < act_ranks)
    def _():
        drain(z1_ref.at[pl.ds(0, n_b - 1)], z1_r)
        z2_ref[za] = add_up(z1_ref)
        for o in range(1, n_a):
            to = yh * n_z + ((za + o) % n_a) * n_b + zb
            send(z2_ref.at[za], z2_ref.at[za], z2_s, z2_r, d, to)

    drain(gpr_ref.at[pl.ds(0, n_dp - 1)], gp_r)
    gpf_ref[rows(d, gp_rows), :] = add_up(gpr_ref)

    def gp_spread(o, _):
        block = gpf_ref.at[rows(d, gp_rows)]
        send(block, block, gpg_s, gpg_r, (d + o) % n_dp, f)
        return 0

    lax.fori_loop(1, n_dp, gp_spread, 0)

    for i in range(2, blocks):
        vg_block(i)

    @pl.when(d < act_ranks)
    def _():
        if n_a > 1:
            drain(z2_ref.at[pl.ds(0, n_a - 1)], z2_r)
        y2_ref[yh] = add_up(z2_ref)
        send(y2_ref.at[yh], y2_ref.at[yh], y2_s, y2_r, d, f_y)
        drain(y2_ref.at[1 - yh], y2_r)
        gmf_ref[rows(d, gm_rows), :] = add_up(y2_ref)
        block = gmf_ref.at[rows(d, gm_rows)]

        def gm_spread(o, _):
            send(block, block, gmg_s, gmg_r, (d + o) % n_dp, f)
            return 0

        lax.fori_loop(1, n_dp, gm_spread, 0)

    drain(gpf_ref.at[pl.ds(0, gp_rows * (n_dp - 1))], gpg_r)
    gp_ref[...] = gpf_ref[...].astype(F32)

    @pl.when(d < act_ranks)
    def _():
        drain(gmf_ref.at[pl.ds(0, gm_rows * (act_ranks - 1))], gmg_r)

    @pl.when(d >= act_ranks)
    def _():
        drain(gmf_ref.at[pl.ds(0, gm_rows * act_ranks)], gmg_r)

    gm_ref[...] = gmf_ref[...].astype(F32)

    drain(v_ref.at[pl.ds(0, dim * (n_f - 1))], a2a_s)

    @pl.when(d == f // per)
    def _():
        drain(w_ref.at[pl.ds(0, dim * (n_f - 1))], w_s)

    drain(wt_ref.at[pl.ds(0, dim * (n_f - per))], wg_s)
    drain(up_ref, up_s)
    drain(dn_ref, dn_s)
    drain(yx_ref.at[0], yx_s)
    drain(hg_ref.at[0], agy_s)
    drain(hg_ref.at[pl.ds(0, 2 * hops_up)], agu_s)
    drain(hg_ref.at[pl.ds(0, 2 * hops_dn)], agd_s)

    @pl.when(d < act_ranks)
    def _():
        drain(gmt_ref.at[pl.ds(0, gm_rows * (act_ranks - 1))], gm_s)
        drain(z1_ref.at[pl.ds(0, n_b - 1)], z1_s)
        if n_a > 1:
            drain(z2_ref.at[pl.ds(0, n_a - 1)], z2_s)
        drain(y2_ref.at[0], y2_s)
        drain(gmr_ref.at[pl.ds(0, n_dp - 1)], gmg_s)

    @pl.when(d >= act_ranks)
    def _():
        drain(gmt_ref.at[pl.ds(0, gm_rows * act_ranks)], gm_s)

    drain(gpt_ref.at[pl.ds(0, gp_rows * (n_dp - 1))], gp_s)
    drain(gpf_ref.at[pl.ds(0, gp_rows * (n_dp - 1))], gpg_s)


def per_device(n_dp, n_f, vectors, labels, pair_weight, hidden_bias, mid_weight, mid_bias, out_weight):
    n_ex, _, _, dim = vectors.shape
    units = pair_weight.shape[3]
    feats = n_f * dim
    share = n_ex // n_f
    n_z = n_f // 2
    hops_up, hops_dn = n_z // 2, n_z // 2 - 1
    gp_rows = feats // n_dp
    gm_rows = 16 * -(-(units + 3) // (16 * n_dp))
    act_ranks = -(-(units + 3) // gm_rows)
    n_b = min(4, n_z)
    n_a = n_z // n_b
    v = jnp.transpose(vectors, (1, 2, 3, 0)).reshape(feats, n_ex)
    vmem = pl.BlockSpec(memory_space=pltpu.VMEM)
    dma = pltpu.SemaphoreType.DMA
    vg, gp, gm = pl.pallas_call(
        functools.partial(kernel, n_dp, n_f, dim, act_ranks),
        out_shape=(
            jax.ShapeDtypeStruct((feats, n_ex), BF16),
            jax.ShapeDtypeStruct((feats, units), F32),
            jax.ShapeDtypeStruct((gm_rows * act_ranks, units), F32),
        ),
        in_specs=[vmem] * 7,
        out_specs=(vmem,) * 3,
        scratch_shapes=[
            pltpu.VMEM((feats, n_ex), BF16),
            pltpu.VMEM((feats, n_ex), BF16),
            pltpu.VMEM((feats, units), BF16),
            pltpu.VMEM((n_f, share, units), F32),
            pltpu.VMEM((2, 2, share, units), BF16),
            pltpu.VMEM((2, hops_up, share, units), BF16),
            pltpu.VMEM((2, hops_dn, share, units), BF16),
            pltpu.VMEM((2, share, units), BF16),
            pltpu.VMEM((n_f, share, units), BF16),
            pltpu.VMEM((gm_rows * act_ranks, units), BF16),
            pltpu.VMEM((n_dp, gm_rows, units), BF16),
            pltpu.VMEM((n_b, gm_rows, units), BF16),
            pltpu.VMEM((n_a, gm_rows, units), BF16),
            pltpu.VMEM((2, gm_rows, units), BF16),
            pltpu.VMEM((gm_rows * act_ranks, units), BF16),
            pltpu.VMEM((feats, units), BF16),
            pltpu.VMEM((n_dp, gp_rows, units), BF16),
            pltpu.VMEM((feats, units), BF16),
            dma((28,)),
            dma((2, hops_up)),
            dma((2, hops_dn)),
            dma((2, hops_up)),
            dma((2, hops_dn)),
        ],
        compiler_params=pltpu.CompilerParams(
            collective_id=0, has_side_effects=True, vmem_limit_bytes=48 * 1024 * 1024
        ),
        name="train_step",
    )(
        v,
        labels.reshape(n_ex // 128, 128),
        pair_weight.reshape(feats, units),
        hidden_bias.reshape(1, units),
        mid_weight,
        mid_bias.reshape(1, units),
        out_weight.reshape(1, units),
    )
    vector_grad = jnp.transpose(vg.reshape(1, n_f, dim, n_ex), (3, 0, 1, 2))
    return (
        vector_grad,
        gp.reshape(1, n_f, dim, units),
        gm[units + 2],
        gm[:units],
        gm[units],
        gm[units + 1],
    )


def solution(mesh):
    in_specs = (
        P("dp", "field", None, None),
        P("dp"),
        P("field", None, None, None),
        P(),
        P(),
        P(),
        P(),
    )
    out_specs = (P("dp", "field", None, None), P("field", None, None, None), P(), P(), P(), P())
    body = functools.partial(per_device, mesh.shape["dp"], mesh.shape["field"])
    return jax.shard_map(body, mesh=mesh, in_specs=in_specs, out_specs=out_specs, check_vma=False)
```

```python
import functools

import jax
import jax.numpy as jnp
from jax import lax
from jax.experimental import pallas as pl
from jax.experimental.pallas import tpu as pltpu
from jax.sharding import PartitionSpec as P

F32 = jnp.float32
BF16 = jnp.bfloat16
MESH = pl.DeviceIdType.MESH


def silu_parts(v):
    s = jax.nn.sigmoid(v)
    return v * s, s * (1.0 + v * (1.0 - s))


def drain(ref, sem):
    pltpu.make_async_copy(ref, ref, sem).wait()


def kernel(
    n_dp, n_f, dim, act_ranks,
    v_ref, lab_ref, w_ref, hb_ref, mw_ref, mb_ref, ow_ref,
    vg_ref, gp_ref, gm_ref,
    slot_ref, p_ref, feat_ref, wt_ref, part_ref, partb_ref, up_ref, dn_ref, yx_ref,
    hg_ref, gmt_ref, gmr_ref, yown_ref, y2_ref, z1_ref, z2_ref, gmf_ref,
    gpt_ref, gpr_ref, gpf_ref,
    one, rs_sem, ag_sem,
):
    (a2a_s, a2a_r, w_s, w_r, wg_s, wg_r, up_s, dn_s, yx_s, yx_r, agu_s, agd_s, agy_s, agy_r,
     gm_s, gm_r, z1_s, z1_r, z2_s, z2_r, y2_s, y2_r, gmg_s, gmg_r, gp_s, gp_r, gpg_s, gpg_r,
     gmy_s, gmy_r) = [
        one.at[i] for i in range(30)]
    n_z = n_f // 2
    steps = n_z // 4
    far = 2 * steps
    d, f = lax.axis_index("dp"), lax.axis_index("field")
    yh, z = f // n_z, f % n_z
    near_f = [yh * n_z + (z + o + n_z) % n_z for o in (1, -1)]
    next_f = [yh * n_z + (z + o + n_z) % n_z for o in (2, -2)]
    f_y = (1 - yh) * n_z + z
    share = part_ref.shape[1]
    units = w_ref.shape[1]
    per = n_f // n_dp

    def send(src, dst, s, r, to_d, to_f):
        pltpu.make_async_remote_copy(
            src_ref=src, dst_ref=dst, send_sem=s, recv_sem=r,
            device_id=(to_d, to_f), device_id_type=MESH,
        ).start()

    def rows(i, n):
        return pl.ds(pl.multiple_of(i * n, n), n)

    barrier = pltpu.get_barrier_semaphore()

    def greet_f(o, _):
        pl.semaphore_signal(barrier, inc=1, device_id=(d, (f + o) % n_f), device_id_type=MESH)
        return 0

    def greet_d(o, _):
        pl.semaphore_signal(barrier, inc=1, device_id=((d + o) % n_dp, f), device_id_type=MESH)
        return 0

    lax.fori_loop(1, n_f, greet_f, 0)
    lax.fori_loop(1, n_dp, greet_d, 0)
    pl.semaphore_wait(barrier, n_f + n_dp - 2)

    half = n_z // 2

    def field(oy, oz):
        return (yh + oy) % 2 * n_z + (z + oz + 2 * n_z) % n_z

    def offsets(r):
        pairs = []
        for k in range(per // 2):
            oz = r * (per // 2) + k
            pairs += [(0, oz), (1, (half - oz + n_z) % n_z)]
        return pairs

    for k, (oy, oz) in enumerate(offsets(d)):
        to = field(oy, oz)
        if k == 0:
            @pl.when(d != 0)
            def _():
                send(w_ref.at[rows(to, dim)], slot_ref.at[rows(d * per + k, dim)], w_s, w_r, d, to)
        else:
            send(w_ref.at[rows(to, dim)], slot_ref.at[rows(d * per + k, dim)], w_s, w_r, d, to)

    def give(oy, oz):
        to = field(oy, oz)
        send(v_ref.at[rows(to, dim)], p_ref.at[rows(f, dim)], a2a_s, a2a_r, d, to)


    def a2a(i, _):
        k = half - i
        for oy in range(2):
            give(oy, k)
            give(oy, -k)
        return 0

    give(0, half)
    give(1, half)
    lax.fori_loop(1, half, a2a, 0)
    give(1, 0)

    p_ref[rows(f, dim), :] = jnp.zeros((dim, p_ref.shape[1]), BF16)

    @pl.when(d == 0)
    def _():
        slot_ref[pl.ds(0, dim), :] = w_ref[rows(f, dim), :]
        drain(slot_ref.at[pl.ds(0, dim * (per - 1))], w_r)

    @pl.when(d != 0)
    def _():
        drain(slot_ref.at[pl.ds(0, dim * per)], w_r)

    def pass_on(o, _):
        block = slot_ref.at[rows(d, dim * per)]
        send(block, block, wg_s, wg_r, (d + o) % n_dp, f)
        return 0

    lax.fori_loop(1, n_dp, pass_on, 0)

    drain(p_ref.at[pl.ds(0, dim * (n_f - 1))], a2a_r)

    n_ex = v_ref.shape[1]
    step = min(256, n_ex)
    for c in range(n_ex // step):
        cols = pl.ds(c * step, step)
        feats = (v_ref[:, cols].astype(F32) * p_ref[:, cols].astype(F32)).astype(BF16)
        feat_ref[:, cols] = feats
        res = lax.dot_general(feats, w_ref[...], (((0,), (0,)), ((), ())), preferred_element_type=F32)
        res = res.reshape(step // share, share, units)
        part_ref[pl.ds(c * step // share, step // share)] = res
        partb_ref[pl.ds(c * step // share, step // share)] = res.astype(BF16)

    sums, sides = (up_ref.at[0], dn_ref.at[0]), (up_ref.at[1], dn_ref.at[1])
    leave = (up_s, dn_s)

    def place_of(y, way, distance):
        return y * n_z + (z + (distance if way == 0 else -distance) + n_z) % n_z

    for y in range(2):
        send(partb_ref.at[place_of(y, 0, far)], sums[0].at[y, 0], up_s, rs_sem.at[0, y, 0], d, next_f[0])
    for s in range(steps):
        for y in range(2):
            for way in range(2):
                send(partb_ref.at[place_of(y, way, far - 1 - 2 * s)], sides[way].at[y, s],
                     leave[way], rs_sem.at[2 + way, y, s], d, near_f[way])

    def stop(y, way, s):
        has_sum = way == 0 or s > 0
        if has_sum:
            drain(sums[way].at[y, s], rs_sem.at[way, y, s])
        drain(sides[way].at[y, s], rs_sem.at[2 + way, y, s])
        acc = sides[way][y, s].astype(F32)
        if has_sum:
            acc = acc + sums[way][y, s].astype(F32)
        return acc

    for s in range(steps - 1):
        for y in range(2):
            for way in range(2):
                acc = stop(y, way, s) + part_ref[place_of(y, way, far - 2 - 2 * s)]
                sides[way][y, s] = acc.astype(BF16)
                send(sides[way].at[y, s], sums[way].at[y, s + 1], leave[way], rs_sem.at[way, y, s + 1], d, next_f[way])

    ends = [part_ref[y * n_z + z] + stop(y, 0, steps - 1) + stop(y, 1, steps - 1) for y in range(2)]

    def total(y):
        return jnp.where(y == 0, ends[0], ends[1])

    yx_ref[0] = total(1 - yh).astype(BF16)
    send(yx_ref.at[0], yx_ref.at[1], yx_s, yx_r, d, f_y)
    mine = total(yh)
    drain(yx_ref.at[1], yx_r)
    pre = mine + yx_ref[1].astype(F32) + hb_ref[...]

    full, slope = silu_parts(pre)
    act = full.astype(BF16)
    mid_pre = jnp.dot(act, mw_ref[...], preferred_element_type=F32) + mb_ref[...]
    mid_act, mid_slope = silu_parts(mid_pre)
    logit = jnp.sum(mid_act * ow_ref[...], axis=1, keepdims=True)
    per_row = 128 // share
    lab = lab_ref[pl.ds(f // per_row, 1), :].astype(F32)
    lane = lax.broadcasted_iota(jnp.int32, (share, 128), 1)
    line = lax.broadcasted_iota(jnp.int32, (share, 128), 0)
    lab = jnp.sum(jnp.where(lane == (f % per_row) * share + line, lab, 0.0), axis=1, keepdims=True)
    lg = jax.nn.sigmoid(logit) - lab
    out_sum = jnp.sum(lg * mid_act, axis=0, keepdims=True)
    mg = (lg * ow_ref[...] * mid_slope).astype(BF16)
    back = lax.dot_general(mg, mw_ref[...], (((1,), (1,)), ((), ())), preferred_element_type=F32)
    hg = (back * slope).astype(BF16)
    hg_ref[f] = hg

    send(hg_ref.at[f], hg_ref.at[f], agy_s, agy_r, d, f_y)
    ag_leave = (agu_s, agd_s)

    def ag_step(k, s):
        base = (yh if k == 0 else 1 - yh) * n_z
        blocks = [hg_ref.at[base + (z - 2 * s + n_z) % n_z], hg_ref.at[base + (z + 2 * s) % n_z]]
        for way in range(2):
            if s > 0:
                drain(blocks[way], ag_sem.at[way, k, s - 1])
            if way == 0 or s < steps - 1:
                send(blocks[way], blocks[way], ag_leave[way], ag_sem.at[way, k, s], d, next_f[way])
            send(blocks[way], blocks[way], ag_leave[way], ag_sem.at[2 + way, k, s], d, near_f[way])

    ag_step(0, 0)

    mid_sum = jnp.sum(mg.astype(F32), axis=0, keepdims=True)
    hid_sum = jnp.sum(hg.astype(F32), axis=0, keepdims=True)
    gmt_ref[pl.ds(0, units), :] = lax.dot_general(
        act, mg, (((0,), (0,)), ((), ())), preferred_element_type=F32).astype(BF16)
    extra = gmt_ref.shape[0] - units
    at = lax.broadcasted_iota(jnp.int32, (extra, units), 0)
    tail = jnp.where(at == 0, mid_sum, jnp.where(at == 1, out_sum, jnp.where(at == 2, hid_sum, 0.0)))
    gmt_ref[pl.ds(units, extra), :] = tail.astype(BF16)
    gm_rows = gmr_ref.shape[1]

    def gm_scatter(o, _):
        to = (d + o) % n_dp

        @pl.when(to < act_ranks)
        def _():
            send(gmt_ref.at[rows(to, gm_rows)], gmr_ref.at[d], gm_s, gm_r, to, f)
        return 0

    lax.fori_loop(1, n_dp, gm_scatter, 0)

    def add_up(ref):
        acc = ref[0].astype(F32)
        for i in range(1, ref.shape[0]):
            acc = acc + ref[i].astype(F32)
        return acc.astype(BF16)

    n_b = z1_ref.shape[0]
    n_a = z2_ref.shape[0]
    za, zb = z // n_b, z % n_b

    def owners_only(task):
        pl.when(d < act_ranks)(task)

    half_rows = gm_rows // 2

    def gm_first():
        gmr_ref[d] = gmt_ref[rows(d, gm_rows), :]
        drain(gmr_ref.at[pl.ds(0, n_dp - 1)], gm_r)
        acc = gmr_ref[0].astype(F32)
        for i in range(1, n_dp):
            acc = acc + gmr_ref[i].astype(F32)
        low, high = acc[:half_rows], acc[half_rows:]
        yown_ref[...] = jnp.where(yh == 0, low, high)
        y2_ref[0] = jnp.where(yh == 0, high, low).astype(BF16)
        send(y2_ref.at[0], y2_ref.at[1], y2_s, y2_r, d, f_y)

    def gm_second():
        drain(y2_ref.at[1], y2_r)
        z1_ref[zb] = (yown_ref[...] + y2_ref[1].astype(F32)).astype(BF16)
        for o in range(1, n_b):
            to = yh * n_z + za * n_b + (zb + o) % n_b
            send(z1_ref.at[zb], z1_ref.at[zb], z1_s, z1_r, d, to)

    def gm_third():
        drain(z1_ref.at[pl.ds(0, n_b - 1)], z1_r)
        z2_ref[za] = add_up(z1_ref)
        for o in range(1, n_a):
            to = yh * n_z + ((za + o) % n_a) * n_b + zb
            send(z2_ref.at[za], z2_ref.at[za], z2_s, z2_r, d, to)

    def gm_fourth():
        if n_a > 1:
            drain(z2_ref.at[pl.ds(0, n_a - 1)], z2_r)
        block = gmf_ref.at[yh, rows(d, half_rows)]
        gmf_ref[yh, rows(d, half_rows), :] = add_up(z2_ref)

        def gm_spread(o, _):
            send(block, block, gmg_s, gmg_r, (d + o) % n_dp, f)
            return 0

        lax.fori_loop(1, n_dp, gm_spread, 0)

    def gm_pair():
        @pl.when(d < act_ranks)
        def _():
            drain(gmf_ref.at[0, pl.ds(0, half_rows * (act_ranks - 1))], gmg_r)

        @pl.when(d >= act_ranks)
        def _():
            drain(gmf_ref.at[0], gmg_r)

        send(gmf_ref.at[yh], gmf_ref.at[yh], gmy_s, gmy_r, d, f_y)

    other = (1 - yh) * n_z + z
    drain(hg_ref.at[other], agy_r)
    ag_step(1, 0)
    for s in range(1, steps):
        for k in range(2):
            ag_step(k, s)
        if s == steps - 2:
            owners_only(gm_first)
    owners_only(gm_second)
    for k in range(2):
        base = (yh if k == 0 else 1 - yh) * n_z
        drain(hg_ref.at[base + (z + n_z - far) % n_z], ag_sem.at[0, k, steps - 1])
        for s in range(steps):
            drain(hg_ref.at[base + (z + n_z - 1 - 2 * s) % n_z], ag_sem.at[2, k, s])
            drain(hg_ref.at[base + (z + 1 + 2 * s) % n_z], ag_sem.at[3, k, s])

    hg_all = hg_ref[...].reshape(n_ex, units)
    gpt_ref[...] = jnp.dot(feat_ref[...], hg_all, preferred_element_type=F32).astype(BF16)
    gp_rows = gpr_ref.shape[1]

    def gp_scatter(o, _):
        to = (d + o) % n_dp
        send(gpt_ref.at[rows(to, gp_rows)], gpr_ref.at[d], gp_s, gp_r, to, f)
        return 0

    lax.fori_loop(1, n_dp, gp_scatter, 0)
    gpr_ref[d] = gpt_ref[rows(d, gp_rows), :]

    drain(slot_ref.at[pl.ds(0, dim * (n_f - per))], wg_r)

    def place(r, _):
        for k, (oy, oz) in enumerate(offsets(r)):
            wt_ref[rows(field(oy, -oz), dim), :] = slot_ref[rows(r * per + k, dim), :]
        return 0

    lax.fori_loop(0, n_dp, place, 0)
    nt = (((1,), (1,)), ((), ()))
    blocks = 4

    def vg_block(i):
        size = v_ref.shape[0] // blocks
        at = pl.ds(i * size, size)
        both = lax.dot_general(w_ref[at, :], hg_all, nt, preferred_element_type=F32)
        both = both + lax.dot_general(wt_ref[at, :], hg_all, nt, preferred_element_type=F32)
        vg_ref[at, :] = (both * p_ref[at, :].astype(F32)).astype(BF16)

    owners_only(gm_third)
    for i in range(blocks // 2):
        vg_block(i)
    owners_only(gm_fourth)

    drain(gpr_ref.at[pl.ds(0, n_dp - 1)], gp_r)
    gpf_ref[rows(d, gp_rows), :] = add_up(gpr_ref)

    def gp_spread(o, _):
        block = gpf_ref.at[rows(d, gp_rows)]
        send(block, block, gpg_s, gpg_r, (d + o) % n_dp, f)
        return 0

    lax.fori_loop(1, n_dp, gp_spread, 0)

    for i in range(blocks // 2, blocks):
        vg_block(i)
    gm_pair()

    drain(gpf_ref.at[pl.ds(0, gp_rows * (n_dp - 1))], gpg_r)
    gp_ref[...] = gpf_ref[...].astype(F32)

    drain(gmf_ref.at[1 - yh], gmy_r)
    for y in range(2):
        gm_ref[:, y] = gmf_ref[y].reshape(act_ranks, half_rows, units).astype(F32)

    drain(v_ref.at[pl.ds(0, dim * (n_f - 1))], a2a_s)


    @pl.when(d == 0)
    def _():
        drain(slot_ref.at[pl.ds(0, dim * (per - 1))], w_s)

    @pl.when(d != 0)
    def _():
        drain(slot_ref.at[pl.ds(0, dim * per)], w_s)

    drain(slot_ref.at[pl.ds(0, dim * per * (n_dp - 1))], wg_s)
    drain(partb_ref.at[pl.ds(0, 2 * far)], up_s)
    drain(partb_ref.at[pl.ds(0, 2 * (far - 1))], dn_s)
    drain(yx_ref.at[0], yx_s)
    drain(hg_ref.at[0], agy_s)
    drain(hg_ref.at[pl.ds(0, 2 * far)], agu_s)
    drain(hg_ref.at[pl.ds(0, 2 * (far - 1))], agd_s)

    @pl.when(d < act_ranks)
    def _():
        drain(gmt_ref.at[pl.ds(0, gm_rows * (act_ranks - 1))], gm_s)
        drain(z1_ref.at[pl.ds(0, n_b - 1)], z1_s)
        if n_a > 1:
            drain(z2_ref.at[pl.ds(0, n_a - 1)], z2_s)
        drain(y2_ref.at[0], y2_s)
        drain(slot_ref.at[pl.ds(0, half_rows * (n_dp - 1))], gmg_s)

    @pl.when(d >= act_ranks)
    def _():
        drain(gmt_ref.at[pl.ds(0, gm_rows * act_ranks)], gm_s)

    drain(gmf_ref.at[0], gmy_s)
    drain(gpt_ref.at[pl.ds(0, gp_rows * (n_dp - 1))], gp_s)
    drain(gpf_ref.at[pl.ds(0, gp_rows * (n_dp - 1))], gpg_s)


def per_device(n_dp, n_f, vectors, labels, pair_weight, hidden_bias, mid_weight, mid_bias, out_weight):
    n_ex, _, _, dim = vectors.shape
    units = pair_weight.shape[3]
    feats = n_f * dim
    share = n_ex // n_f
    n_z = n_f // 2
    steps = n_z // 4
    gp_rows = feats // n_dp
    gm_rows = 16 * -(-(units + 3) // (16 * n_dp))
    act_ranks = -(-(units + 3) // gm_rows)
    n_b = min(4, n_z)
    n_a = n_z // n_b
    v = jnp.transpose(vectors, (1, 2, 3, 0)).reshape(feats, n_ex)
    vmem = pl.BlockSpec(memory_space=pltpu.VMEM)
    dma = pltpu.SemaphoreType.DMA
    vg, gp, gm = pl.pallas_call(
        functools.partial(kernel, n_dp, n_f, dim, act_ranks),
        out_shape=(
            jax.ShapeDtypeStruct((feats, n_ex), BF16),
            jax.ShapeDtypeStruct((feats, units), F32),
            jax.ShapeDtypeStruct((act_ranks, 2, gm_rows // 2, units), F32),
        ),
        in_specs=[vmem] * 7,
        out_specs=(vmem,) * 3,
        scratch_shapes=[
            pltpu.VMEM((feats, units), BF16),
            pltpu.VMEM((feats, n_ex), BF16),
            pltpu.VMEM((feats, n_ex), BF16),
            pltpu.VMEM((feats, units), BF16),
            pltpu.VMEM((n_f, share, units), F32),
            pltpu.VMEM((n_f, share, units), BF16),
            pltpu.VMEM((2, 2, steps, share, units), BF16),
            pltpu.VMEM((2, 2, steps, share, units), BF16),
            pltpu.VMEM((2, share, units), BF16),
            pltpu.VMEM((n_f, share, units), BF16),
            pltpu.VMEM((gm_rows * act_ranks, units), BF16),
            pltpu.VMEM((n_dp, gm_rows, units), BF16),
            pltpu.VMEM((gm_rows // 2, units), F32),
            pltpu.VMEM((2, gm_rows // 2, units), BF16),
            pltpu.VMEM((n_b, gm_rows // 2, units), BF16),
            pltpu.VMEM((n_a, gm_rows // 2, units), BF16),
            pltpu.VMEM((2, gm_rows // 2 * act_ranks, units), BF16),
            pltpu.VMEM((feats, units), BF16),
            pltpu.VMEM((n_dp, gp_rows, units), BF16),
            pltpu.VMEM((feats, units), BF16),
            dma((30,)),
            dma((4, 2, steps)),
            dma((4, 2, steps)),
        ],
        compiler_params=pltpu.CompilerParams(
            collective_id=0, has_side_effects=True, vmem_limit_bytes=48 * 1024 * 1024
        ),
        name="train_step",
    )(
        v,
        labels.reshape(n_ex // 128, 128),
        pair_weight.reshape(feats, units),
        hidden_bias.reshape(1, units),
        mid_weight,
        mid_bias.reshape(1, units),
        out_weight.reshape(1, units),
    )
    gm = gm.reshape(act_ranks * gm_rows, units)
    vector_grad = jnp.transpose(vg.reshape(1, n_f, dim, n_ex), (3, 0, 1, 2))
    return (
        vector_grad,
        gp.reshape(1, n_f, dim, units),
        gm[units + 2],
        gm[:units],
        gm[units],
        gm[units + 1],
    )


def solution(mesh):
    in_specs = (
        P("dp", "field", None, None),
        P("dp"),
        P("field", None, None, None),
        P(),
        P(),
        P(),
        P(),
    )
    out_specs = (P("dp", "field", None, None), P("field", None, None, None), P(), P(), P(), P())
    body = functools.partial(per_device, mesh.shape["dp"], mesh.shape["field"])
    return jax.shard_map(body, mesh=mesh, in_specs=in_specs, out_specs=out_specs, check_vma=False)
```

```python
import functools

import jax
import jax.numpy as jnp
from jax import lax
from jax.experimental import pallas as pl
from jax.experimental.pallas import tpu as pltpu
from jax.sharding import PartitionSpec as P

F32 = jnp.float32
BF16 = jnp.bfloat16
MESH = pl.DeviceIdType.MESH


def silu_parts(v):
    s = jax.nn.sigmoid(v)
    return v * s, s * (1.0 + v * (1.0 - s))


def drain(ref, sem):
    pltpu.make_async_copy(ref, ref, sem).wait()


def kernel(
    n_dp, n_f, dim, act_ranks,
    v_ref, lab_ref, w_ref, hb_ref, mw_ref, mb_ref, ow_ref,
    vg_ref, gp_ref, gm_ref,
    slot_ref, p_ref, feat_ref, wt_ref, part_ref, partb_ref, up_ref, dn_ref, yx_ref,
    hg_ref, gmt_ref, gmr_ref, yown_ref, y2_ref, z1_ref, z2_ref, gmf_ref,
    gpt_ref, gpr_ref, gpf_ref,
    one, rs_sem, ag_sem,
):
    (a2a_s, a2a_r, w_s, w_r, wg_s, wg_r, up_s, dn_s, yx_s, yx_r, agu_s, agd_s, agy_s, agy_r,
     gm_s, gm_r, z1_s, z1_r, z2_s, z2_r, y2_s, y2_r, gmg_s, gmg_r, gp_s, gp_r, gpg_s, gpg_r,
     gmy_s, gmy_r) = [
        one.at[i] for i in range(30)]
    n_z = n_f // 2
    steps = n_z // 4
    far = 2 * steps
    d, f = lax.axis_index("dp"), lax.axis_index("field")
    yh, z = f // n_z, f % n_z
    near_f = [yh * n_z + (z + o + n_z) % n_z for o in (1, -1)]
    next_f = [yh * n_z + (z + o + n_z) % n_z for o in (2, -2)]
    f_y = (1 - yh) * n_z + z
    share = part_ref.shape[1]
    units = w_ref.shape[1]
    per = n_f // n_dp

    def send(src, dst, s, r, to_d, to_f):
        pltpu.make_async_remote_copy(
            src_ref=src, dst_ref=dst, send_sem=s, recv_sem=r,
            device_id=(to_d, to_f), device_id_type=MESH,
        ).start()

    def rows(i, n):
        return pl.ds(pl.multiple_of(i * n, n), n)

    barrier = pltpu.get_barrier_semaphore()

    def greet_f(o, _):
        pl.semaphore_signal(barrier, inc=1, device_id=(d, (f + o) % n_f), device_id_type=MESH)
        return 0

    def greet_d(o, _):
        pl.semaphore_signal(barrier, inc=1, device_id=((d + o) % n_dp, f), device_id_type=MESH)
        return 0

    lax.fori_loop(1, n_f, greet_f, 0)
    lax.fori_loop(1, n_dp, greet_d, 0)
    pl.semaphore_wait(barrier, n_f + n_dp - 2)

    half = n_z // 2

    def field(oy, oz):
        return (yh + oy) % 2 * n_z + (z + oz + 2 * n_z) % n_z

    def offsets(r):
        pairs = []
        for k in range(per // 2):
            oz = r * (per // 2) + k
            pairs += [(0, oz), (1, (half - oz + n_z) % n_z)]
        return pairs

    for k, (oy, oz) in enumerate(offsets(d)):
        to = field(oy, oz)
        if k == 0:
            @pl.when(d != 0)
            def _():
                send(w_ref.at[rows(to, dim)], slot_ref.at[rows(d * per + k, dim)], w_s, w_r, d, to)
        else:
            send(w_ref.at[rows(to, dim)], slot_ref.at[rows(d * per + k, dim)], w_s, w_r, d, to)

    def give(oy, oz):
        to = field(oy, oz)
        send(v_ref.at[rows(to, dim)], p_ref.at[rows(f, dim)], a2a_s, a2a_r, d, to)


    def a2a(i, _):
        k = half - i
        for oy in range(2):
            give(oy, k)
            give(oy, -k)
        return 0

    give(0, half)
    give(1, half)
    lax.fori_loop(1, half, a2a, 0)
    give(1, 0)

    p_ref[rows(f, dim), :] = jnp.zeros((dim, p_ref.shape[1]), BF16)

    @pl.when(d == 0)
    def _():
        slot_ref[pl.ds(0, dim), :] = w_ref[rows(f, dim), :]
        drain(slot_ref.at[pl.ds(0, dim * (per - 1))], w_r)

    @pl.when(d != 0)
    def _():
        drain(slot_ref.at[pl.ds(0, dim * per)], w_r)

    def pass_on(o, _):
        block = slot_ref.at[rows(d, dim * per)]
        send(block, block, wg_s, wg_r, (d + o) % n_dp, f)
        return 0

    lax.fori_loop(1, n_dp, pass_on, 0)

    drain(p_ref.at[pl.ds(0, dim * (n_f - 1))], a2a_r)

    n_ex = v_ref.shape[1]
    step = min(256, n_ex)
    for c in range(n_ex // step):
        cols = pl.ds(c * step, step)
        feats = (v_ref[:, cols].astype(F32) * p_ref[:, cols].astype(F32)).astype(BF16)
        feat_ref[:, cols] = feats
        res = lax.dot_general(feats, w_ref[...], (((0,), (0,)), ((), ())), preferred_element_type=F32)
        res = res.reshape(step // share, share, units)
        part_ref[pl.ds(c * step // share, step // share)] = res
        partb_ref[pl.ds(c * step // share, step // share)] = res.astype(BF16)

    sums, sides = (up_ref.at[0], dn_ref.at[0]), (up_ref.at[1], dn_ref.at[1])
    leave = (up_s, dn_s)

    def place_of(y, way, distance):
        return y * n_z + (z + (distance if way == 0 else -distance) + n_z) % n_z

    def aim(y, s, offset):
        if s < steps - 1:
            return y, yh * n_z + (z + offset + n_z) % n_z
        return (y + yh) % 2, y * n_z + (z + offset + n_z) % n_z

    def send_sides(s):
        for y in range(2):
            for way in range(2):
                slot, to = aim(y, s, (1, -1)[way])
                send(partb_ref.at[place_of(y, way, far - 1 - 2 * s)], sides[way].at[slot, s],
                     leave[way], rs_sem.at[2 + way, slot, s], d, to)

    for y in range(2):
        slot, to = aim(y, 0, 2)
        send(partb_ref.at[place_of(y, 0, far)], sums[0].at[slot, 0], up_s, rs_sem.at[0, slot, 0], d, to)
    send_sides(0)
    send_sides(1)
    send(partb_ref.at[f_y], yx_ref, yx_s, yx_r, d, f_y)

    def stop(y, way, s):
        has_sum = way == 0 or s > 0
        if has_sum:
            drain(sums[way].at[y, s], rs_sem.at[way, y, s])
        drain(sides[way].at[y, s], rs_sem.at[2 + way, y, s])
        acc = sides[way][y, s].astype(F32)
        if has_sum:
            acc = acc + sums[way][y, s].astype(F32)
        return acc

    for s in range(steps - 1):
        for y in range(2):
            for way in range(2):
                acc = stop(y, way, s) + part_ref[place_of(y, way, far - 2 - 2 * s)]
                sides[way][y, s] = acc.astype(BF16)
                slot, to = aim(y, s + 1, (2, -2)[way])
                send(sides[way].at[y, s], sums[way].at[slot, s + 1], leave[way], rs_sem.at[way, slot, s + 1], d, to)
        if s + 2 < steps:
            send_sides(s + 2)

    drain(yx_ref, yx_r)
    pre = part_ref[f] + yx_ref[...].astype(F32) + hb_ref[...]
    for k in range(2):
        for way in range(2):
            pre = pre + stop(k, way, steps - 1)

    full, slope = silu_parts(pre)
    act = full.astype(BF16)
    mid_pre = jnp.dot(act, mw_ref[...], preferred_element_type=F32) + mb_ref[...]
    mid_act, mid_slope = silu_parts(mid_pre)
    logit = jnp.sum(mid_act * ow_ref[...], axis=1, keepdims=True)
    per_row = 128 // share
    lab = lab_ref[pl.ds(f // per_row, 1), :].astype(F32)
    lane = lax.broadcasted_iota(jnp.int32, (share, 128), 1)
    line = lax.broadcasted_iota(jnp.int32, (share, 128), 0)
    lab = jnp.sum(jnp.where(lane == (f % per_row) * share + line, lab, 0.0), axis=1, keepdims=True)
    lg = jax.nn.sigmoid(logit) - lab
    out_sum = jnp.sum(lg * mid_act, axis=0, keepdims=True)
    mg = (lg * ow_ref[...] * mid_slope).astype(BF16)
    back = lax.dot_general(mg, mw_ref[...], (((1,), (1,)), ((), ())), preferred_element_type=F32)
    hg = (back * slope).astype(BF16)
    hg_ref[f] = hg

    ag_leave = (agu_s, agd_s)

    def ag_step(k, s):
        base = (yh if k == 0 else 1 - yh) * n_z
        blocks = [hg_ref.at[base + (z - 2 * s + n_z) % n_z], hg_ref.at[base + (z + 2 * s) % n_z]]
        for way in range(2):
            if s > 0:
                drain(blocks[way], ag_sem.at[way, k, s - 1])
            if way == 0 or s < steps - 1:
                send(blocks[way], blocks[way], ag_leave[way], ag_sem.at[way, k, s], d, next_f[way])
            send(blocks[way], blocks[way], ag_leave[way], ag_sem.at[2 + way, k, s], d, near_f[way])

    ag_step(0, 0)
    for way in range(2):
        cross = [(1 - yh) * n_z + (z + o + n_z) % n_z for o in ((2, 1), (-2, -1))[way]]
        send(hg_ref.at[f], hg_ref.at[f], ag_leave[way], ag_sem.at[way, 1, 0], d, cross[0])
        send(hg_ref.at[f], hg_ref.at[f], ag_leave[way], ag_sem.at[2 + way, 1, 0], d, cross[1])
    send(hg_ref.at[f], hg_ref.at[f], agy_s, agy_r, d, f_y)

    mid_sum = jnp.sum(mg.astype(F32), axis=0, keepdims=True)
    hid_sum = jnp.sum(hg.astype(F32), axis=0, keepdims=True)
    gmt_ref[pl.ds(0, units), :] = lax.dot_general(
        act, mg, (((0,), (0,)), ((), ())), preferred_element_type=F32).astype(BF16)
    extra = gmt_ref.shape[0] - units
    at = lax.broadcasted_iota(jnp.int32, (extra, units), 0)
    tail = jnp.where(at == 0, mid_sum, jnp.where(at == 1, out_sum, jnp.where(at == 2, hid_sum, 0.0)))
    gmt_ref[pl.ds(units, extra), :] = tail.astype(BF16)
    gm_rows = gmr_ref.shape[1]

    def gm_scatter(o, _):
        to = (d + o) % n_dp

        @pl.when(to < act_ranks)
        def _():
            send(gmt_ref.at[rows(to, gm_rows)], gmr_ref.at[d], gm_s, gm_r, to, f)
        return 0

    lax.fori_loop(1, n_dp, gm_scatter, 0)

    def add_up(ref):
        acc = ref[0].astype(F32)
        for i in range(1, ref.shape[0]):
            acc = acc + ref[i].astype(F32)
        return acc.astype(BF16)

    n_b = z1_ref.shape[0]
    n_a = z2_ref.shape[0]
    za, zb = z // n_b, z % n_b

    def owners_only(task):
        pl.when(d < act_ranks)(task)

    half_rows = gm_rows // 2

    def gm_first():
        gmr_ref[d] = gmt_ref[rows(d, gm_rows), :]
        drain(gmr_ref.at[pl.ds(0, n_dp - 1)], gm_r)
        acc = gmr_ref[0].astype(F32)
        for i in range(1, n_dp):
            acc = acc + gmr_ref[i].astype(F32)
        low, high = acc[:half_rows], acc[half_rows:]
        yown_ref[...] = jnp.where(yh == 0, low, high)
        y2_ref[0] = jnp.where(yh == 0, high, low).astype(BF16)
        send(y2_ref.at[0], y2_ref.at[1], y2_s, y2_r, d, f_y)

    def gm_second():
        drain(y2_ref.at[1], y2_r)
        z1_ref[zb] = (yown_ref[...] + y2_ref[1].astype(F32)).astype(BF16)
        for o in range(1, n_b):
            to = yh * n_z + za * n_b + (zb + o) % n_b
            send(z1_ref.at[zb], z1_ref.at[zb], z1_s, z1_r, d, to)

    def gm_third():
        drain(z1_ref.at[pl.ds(0, n_b - 1)], z1_r)
        z2_ref[za] = add_up(z1_ref)
        for o in range(1, n_a):
            to = yh * n_z + ((za + o) % n_a) * n_b + zb
            send(z2_ref.at[za], z2_ref.at[za], z2_s, z2_r, d, to)

    def gm_fourth():
        if n_a > 1:
            drain(z2_ref.at[pl.ds(0, n_a - 1)], z2_r)
        block = gmf_ref.at[yh, rows(d, half_rows)]
        gmf_ref[yh, rows(d, half_rows), :] = add_up(z2_ref)

        def gm_spread(o, _):
            send(block, block, gmg_s, gmg_r, (d + o) % n_dp, f)
            return 0

        lax.fori_loop(1, n_dp, gm_spread, 0)

    def gm_pair():
        @pl.when(d < act_ranks)
        def _():
            drain(gmf_ref.at[0, pl.ds(0, half_rows * (act_ranks - 1))], gmg_r)

        @pl.when(d >= act_ranks)
        def _():
            drain(gmf_ref.at[0], gmg_r)

        send(gmf_ref.at[yh], gmf_ref.at[yh], gmy_s, gmy_r, d, f_y)

    for s in range(1, steps):
        for k in range(2):
            ag_step(k, s)
        if s == steps - 2:
            owners_only(gm_first)
    owners_only(gm_second)
    drain(hg_ref.at[f_y], agy_r)
    for k in range(2):
        base = (yh if k == 0 else 1 - yh) * n_z
        drain(hg_ref.at[base + (z + n_z - far) % n_z], ag_sem.at[0, k, steps - 1])
        for s in range(steps):
            drain(hg_ref.at[base + (z + n_z - 1 - 2 * s) % n_z], ag_sem.at[2, k, s])
            drain(hg_ref.at[base + (z + 1 + 2 * s) % n_z], ag_sem.at[3, k, s])
    owners_only(gm_third)

    hg_all = hg_ref[...].reshape(n_ex, units)
    gpt_ref[...] = jnp.dot(feat_ref[...], hg_all, preferred_element_type=F32).astype(BF16)
    gp_rows = gpr_ref.shape[1]

    def gp_scatter(o, _):
        to = (d + o) % n_dp
        send(gpt_ref.at[rows(to, gp_rows)], gpr_ref.at[d], gp_s, gp_r, to, f)
        return 0

    lax.fori_loop(1, n_dp, gp_scatter, 0)
    gpr_ref[d] = gpt_ref[rows(d, gp_rows), :]

    drain(slot_ref.at[pl.ds(0, dim * (n_f - per))], wg_r)

    def place(r, _):
        for k, (oy, oz) in enumerate(offsets(r)):
            wt_ref[rows(field(oy, -oz), dim), :] = slot_ref[rows(r * per + k, dim), :]
        return 0

    lax.fori_loop(0, n_dp, place, 0)
    nt = (((1,), (1,)), ((), ()))
    blocks = 4

    def vg_block(i):
        size = v_ref.shape[0] // blocks
        at = pl.ds(i * size, size)
        both = lax.dot_general(w_ref[at, :], hg_all, nt, preferred_element_type=F32)
        both = both + lax.dot_general(wt_ref[at, :], hg_all, nt, preferred_element_type=F32)
        vg_ref[at, :] = (both * p_ref[at, :].astype(F32)).astype(BF16)

    for i in range(blocks // 2):
        vg_block(i)
    owners_only(gm_fourth)

    drain(gpr_ref.at[pl.ds(0, n_dp - 1)], gp_r)
    gpf_ref[rows(d, gp_rows), :] = add_up(gpr_ref)

    def gp_spread(o, _):
        block = gpf_ref.at[rows(d, gp_rows)]
        send(block, block, gpg_s, gpg_r, (d + o) % n_dp, f)
        return 0

    lax.fori_loop(1, n_dp, gp_spread, 0)

    for i in range(blocks // 2, blocks):
        vg_block(i)
    gm_pair()

    drain(gpf_ref.at[pl.ds(0, gp_rows * (n_dp - 1))], gpg_r)
    gp_ref[...] = gpf_ref[...].astype(F32)

    drain(gmf_ref.at[1 - yh], gmy_r)
    for y in range(2):
        gm_ref[:, y] = gmf_ref[y].reshape(act_ranks, half_rows, units).astype(F32)

    drain(v_ref.at[pl.ds(0, dim * (n_f - 1))], a2a_s)


    @pl.when(d == 0)
    def _():
        drain(slot_ref.at[pl.ds(0, dim * (per - 1))], w_s)

    @pl.when(d != 0)
    def _():
        drain(slot_ref.at[pl.ds(0, dim * per)], w_s)

    drain(slot_ref.at[pl.ds(0, dim * per * (n_dp - 1))], wg_s)
    drain(partb_ref.at[pl.ds(0, 2 * far)], up_s)
    drain(partb_ref.at[pl.ds(0, 2 * (far - 1))], dn_s)
    drain(yx_ref, yx_s)
    drain(hg_ref.at[0], agy_s)
    drain(hg_ref.at[pl.ds(0, 2 * far)], agu_s)
    drain(hg_ref.at[pl.ds(0, 2 * (far - 1))], agd_s)

    @pl.when(d < act_ranks)
    def _():
        drain(gmt_ref.at[pl.ds(0, gm_rows * (act_ranks - 1))], gm_s)
        drain(z1_ref.at[pl.ds(0, n_b - 1)], z1_s)
        if n_a > 1:
            drain(z2_ref.at[pl.ds(0, n_a - 1)], z2_s)
        drain(y2_ref.at[0], y2_s)
        drain(slot_ref.at[pl.ds(0, half_rows * (n_dp - 1))], gmg_s)

    @pl.when(d >= act_ranks)
    def _():
        drain(gmt_ref.at[pl.ds(0, gm_rows * act_ranks)], gm_s)

    drain(gmf_ref.at[0], gmy_s)
    drain(gpt_ref.at[pl.ds(0, gp_rows * (n_dp - 1))], gp_s)
    drain(gpf_ref.at[pl.ds(0, gp_rows * (n_dp - 1))], gpg_s)


def per_device(n_dp, n_f, vectors, labels, pair_weight, hidden_bias, mid_weight, mid_bias, out_weight):
    n_ex, _, _, dim = vectors.shape
    units = pair_weight.shape[3]
    feats = n_f * dim
    share = n_ex // n_f
    n_z = n_f // 2
    steps = n_z // 4
    gp_rows = feats // n_dp
    gm_rows = 16 * -(-(units + 3) // (16 * n_dp))
    act_ranks = -(-(units + 3) // gm_rows)
    n_b = min(4, n_z)
    n_a = n_z // n_b
    v = jnp.transpose(vectors, (1, 2, 3, 0)).reshape(feats, n_ex)
    vmem = pl.BlockSpec(memory_space=pltpu.VMEM)
    dma = pltpu.SemaphoreType.DMA
    vg, gp, gm = pl.pallas_call(
        functools.partial(kernel, n_dp, n_f, dim, act_ranks),
        out_shape=(
            jax.ShapeDtypeStruct((feats, n_ex), BF16),
            jax.ShapeDtypeStruct((feats, units), F32),
            jax.ShapeDtypeStruct((act_ranks, 2, gm_rows // 2, units), F32),
        ),
        in_specs=[vmem] * 7,
        out_specs=(vmem,) * 3,
        scratch_shapes=[
            pltpu.VMEM((feats, units), BF16),
            pltpu.VMEM((feats, n_ex), BF16),
            pltpu.VMEM((feats, n_ex), BF16),
            pltpu.VMEM((feats, units), BF16),
            pltpu.VMEM((n_f, share, units), F32),
            pltpu.VMEM((n_f, share, units), BF16),
            pltpu.VMEM((2, 2, steps, share, units), BF16),
            pltpu.VMEM((2, 2, steps, share, units), BF16),
            pltpu.VMEM((share, units), BF16),
            pltpu.VMEM((n_f, share, units), BF16),
            pltpu.VMEM((gm_rows * act_ranks, units), BF16),
            pltpu.VMEM((n_dp, gm_rows, units), BF16),
            pltpu.VMEM((gm_rows // 2, units), F32),
            pltpu.VMEM((2, gm_rows // 2, units), BF16),
            pltpu.VMEM((n_b, gm_rows // 2, units), BF16),
            pltpu.VMEM((n_a, gm_rows // 2, units), BF16),
            pltpu.VMEM((2, gm_rows // 2 * act_ranks, units), BF16),
            pltpu.VMEM((feats, units), BF16),
            pltpu.VMEM((n_dp, gp_rows, units), BF16),
            pltpu.VMEM((feats, units), BF16),
            dma((30,)),
            dma((4, 2, steps)),
            dma((4, 2, steps)),
        ],
        compiler_params=pltpu.CompilerParams(
            collective_id=0, has_side_effects=True, vmem_limit_bytes=48 * 1024 * 1024
        ),
        name="train_step",
    )(
        v,
        labels.reshape(n_ex // 128, 128),
        pair_weight.reshape(feats, units),
        hidden_bias.reshape(1, units),
        mid_weight,
        mid_bias.reshape(1, units),
        out_weight.reshape(1, units),
    )
    gm = gm.reshape(act_ranks * gm_rows, units)
    vector_grad = jnp.transpose(vg.reshape(1, n_f, dim, n_ex), (3, 0, 1, 2))
    return (
        vector_grad,
        gp.reshape(1, n_f, dim, units),
        gm[units + 2],
        gm[:units],
        gm[units],
        gm[units + 1],
    )


def solution(mesh):
    in_specs = (
        P("dp", "field", None, None),
        P("dp"),
        P("field", None, None, None),
        P(),
        P(),
        P(),
        P(),
    )
    out_specs = (P("dp", "field", None, None), P("field", None, None, None), P(), P(), P(), P())
    body = functools.partial(per_device, mesh.shape["dp"], mesh.shape["field"])
    return jax.shard_map(body, mesh=mesh, in_specs=in_specs, out_specs=out_specs, check_vma=False)
```

```python
import functools

import jax
import jax.numpy as jnp
from jax import lax
from jax.experimental import pallas as pl
from jax.experimental.pallas import tpu as pltpu
from jax.sharding import PartitionSpec as P

F32 = jnp.float32
BF16 = jnp.bfloat16
MESH = pl.DeviceIdType.MESH


def silu_parts(v):
    s = jax.nn.sigmoid(v)
    return v * s, s * (1.0 + v * (1.0 - s))


def drain(ref, sem):
    pltpu.make_async_copy(ref, ref, sem).wait()


def kernel(
    n_dp, n_f, dim, act_ranks,
    v_ref, lab_ref, w_ref, hb_ref, mw_ref, mb_ref, ow_ref,
    vg_ref, gp_ref, gm_ref,
    slot_ref, p_ref, feat_ref, wt_ref, part_ref, partb_ref, up_ref, dn_ref, yx_ref,
    hg_ref, gmt_ref, gmr_ref, yown_ref, y2_ref, z1_ref, z2_ref, gmf_ref,
    gpt_ref, gpr_ref, gpf_ref,
    one, rs_sem, ag_sem,
):
    (a2a_s, a2a_r, w_s, w_r, wg_s, wg_r, up_s, dn_s, yx_s, yx_r, agu_s, agd_s, agy_s, agy_r,
     gm_s, gm_r, z1_s, z1_r, z2_s, z2_r, y2_s, y2_r, gmg_s, gmg_r, gp_s, gp_r, gpg_s, gpg_r,
     gmy_s, gmy_r) = [
        one.at[i] for i in range(30)]
    n_z = n_f // 2
    steps = n_z // 4
    far = 2 * steps
    d, f = lax.axis_index("dp"), lax.axis_index("field")
    yh, z = f // n_z, f % n_z
    near_f = [yh * n_z + (z + o + n_z) % n_z for o in (1, -1)]
    next_f = [yh * n_z + (z + o + n_z) % n_z for o in (2, -2)]
    f_y = (1 - yh) * n_z + z
    share = part_ref.shape[1]
    units = w_ref.shape[1]
    per = n_f // n_dp

    def send(src, dst, s, r, to_d, to_f):
        pltpu.make_async_remote_copy(
            src_ref=src, dst_ref=dst, send_sem=s, recv_sem=r,
            device_id=(to_d, to_f), device_id_type=MESH,
        ).start()

    def rows(i, n):
        return pl.ds(pl.multiple_of(i * n, n), n)

    barrier = pltpu.get_barrier_semaphore()

    def greet_f(o, _):
        pl.semaphore_signal(barrier, inc=1, device_id=(d, (f + o) % n_f), device_id_type=MESH)
        return 0

    def greet_d(o, _):
        pl.semaphore_signal(barrier, inc=1, device_id=((d + o) % n_dp, f), device_id_type=MESH)
        return 0

    lax.fori_loop(1, n_f, greet_f, 0)
    lax.fori_loop(1, n_dp, greet_d, 0)
    pl.semaphore_wait(barrier, n_f + n_dp - 2)

    half = n_z // 2

    def field(oy, oz):
        return (yh + oy) % 2 * n_z + (z + oz + 2 * n_z) % n_z

    def offsets(r):
        pairs = []
        for k in range(per // 2):
            oz = r * (per // 2) + k
            pairs += [(0, oz), (1, (half - oz + n_z) % n_z)]
        return pairs

    for k, (oy, oz) in enumerate(offsets(d)):
        to = field(oy, oz)
        if k == 0:
            @pl.when(d != 0)
            def _():
                send(w_ref.at[rows(to, dim)], slot_ref.at[rows(d * per + k, dim)], w_s, w_r, d, to)
        else:
            send(w_ref.at[rows(to, dim)], slot_ref.at[rows(d * per + k, dim)], w_s, w_r, d, to)

    def give(oy, oz):
        to = field(oy, oz)
        send(v_ref.at[rows(to, dim)], p_ref.at[rows(f, dim)], a2a_s, a2a_r, d, to)


    def a2a(i, _):
        k = half - i
        for oy in range(2):
            give(oy, k)
            give(oy, -k)
        return 0

    give(0, half)
    give(1, half)
    lax.fori_loop(1, half, a2a, 0)
    give(1, 0)

    p_ref[rows(f, dim), :] = jnp.zeros((dim, p_ref.shape[1]), BF16)

    @pl.when(d == 0)
    def _():
        slot_ref[pl.ds(0, dim), :] = w_ref[rows(f, dim), :]
        drain(slot_ref.at[pl.ds(0, dim * (per - 1))], w_r)

    @pl.when(d != 0)
    def _():
        drain(slot_ref.at[pl.ds(0, dim * per)], w_r)

    def pass_on(o, _):
        block = slot_ref.at[rows(d, dim * per)]
        send(block, block, wg_s, wg_r, (d + o) % n_dp, f)
        return 0

    lax.fori_loop(1, n_dp, pass_on, 0)

    drain(p_ref.at[pl.ds(0, dim * (n_f - 1))], a2a_r)

    n_ex = v_ref.shape[1]
    step = min(256, n_ex)
    for c in range(n_ex // step):
        cols = pl.ds(c * step, step)
        feats = (v_ref[:, cols].astype(F32) * p_ref[:, cols].astype(F32)).astype(BF16)
        feat_ref[:, cols] = feats
        res = lax.dot_general(feats, w_ref[...], (((0,), (0,)), ((), ())), preferred_element_type=F32)
        res = res.reshape(step // share, share, units)
        part_ref[pl.ds(c * step // share, step // share)] = res
        partb_ref[pl.ds(c * step // share, step // share)] = res.astype(BF16)

    sums, sides = (up_ref.at[0], dn_ref.at[0]), (up_ref.at[1], dn_ref.at[1])
    leave = (up_s, dn_s)

    def place_of(y, way, distance):
        return y * n_z + (z + (distance if way == 0 else -distance) + n_z) % n_z

    def aim(y, s, offset):
        if s < steps - 1:
            return y, yh * n_z + (z + offset + n_z) % n_z
        return (y + yh) % 2, y * n_z + (z + offset + n_z) % n_z

    def send_sides(s):
        for y in range(2):
            for way in range(2):
                slot, to = aim(y, s, (1, -1)[way])
                send(partb_ref.at[place_of(y, way, far - 1 - 2 * s)], sides[way].at[slot, s],
                     leave[way], rs_sem.at[2 + way, slot, s], d, to)

    for y in range(2):
        slot, to = aim(y, 0, 2)
        send(partb_ref.at[place_of(y, 0, far)], sums[0].at[slot, 0], up_s, rs_sem.at[0, slot, 0], d, to)
    send_sides(0)
    send_sides(1)
    send(partb_ref.at[f_y], yx_ref, yx_s, yx_r, d, f_y)

    def stop(y, way, s):
        has_sum = way == 0 or s > 0
        if has_sum:
            drain(sums[way].at[y, s], rs_sem.at[way, y, s])
        drain(sides[way].at[y, s], rs_sem.at[2 + way, y, s])
        acc = sides[way][y, s].astype(F32)
        if has_sum:
            acc = acc + sums[way][y, s].astype(F32)
        return acc

    for s in range(steps - 1):
        for y in range(2):
            for way in range(2):
                acc = stop(y, way, s) + part_ref[place_of(y, way, far - 2 - 2 * s)]
                sides[way][y, s] = acc.astype(BF16)
                slot, to = aim(y, s + 1, (2, -2)[way])
                send(sides[way].at[y, s], sums[way].at[slot, s + 1], leave[way], rs_sem.at[way, slot, s + 1], d, to)
        if s + 2 < steps:
            send_sides(s + 2)

    drain(yx_ref, yx_r)
    pre = part_ref[f] + yx_ref[...].astype(F32) + hb_ref[...]
    for k in range(2):
        for way in range(2):
            pre = pre + stop(k, way, steps - 1)

    full, slope = silu_parts(pre)
    act = full.astype(BF16)
    mid_pre = jnp.dot(act, mw_ref[...], preferred_element_type=F32) + mb_ref[...]
    mid_act, mid_slope = silu_parts(mid_pre)
    logit = jnp.sum(mid_act * ow_ref[...], axis=1, keepdims=True)
    per_row = 128 // share
    lab = lab_ref[pl.ds(f // per_row, 1), :].astype(F32)
    lane = lax.broadcasted_iota(jnp.int32, (share, 128), 1)
    line = lax.broadcasted_iota(jnp.int32, (share, 128), 0)
    lab = jnp.sum(jnp.where(lane == (f % per_row) * share + line, lab, 0.0), axis=1, keepdims=True)
    lg = jax.nn.sigmoid(logit) - lab
    out_sum = jnp.sum(lg * mid_act, axis=0, keepdims=True)
    mg = (lg * ow_ref[...] * mid_slope).astype(BF16)
    back = lax.dot_general(mg, mw_ref[...], (((1,), (1,)), ((), ())), preferred_element_type=F32)
    hg = (back * slope).astype(BF16)
    hg_ref[f] = hg

    ag_leave = (agu_s, agd_s)

    def ag_step(s):
        todo = []
        for k in range(2):
            base = (yh if k == 0 else 1 - yh) * n_z
            for way in range(2):
                block = hg_ref.at[base + (z + (-2 * s, 2 * s)[way] + n_z) % n_z]
                drain(block, ag_sem.at[way, k, s - 1])
                if way == 0 or s < steps - 1:
                    send(block, block, ag_leave[way], ag_sem.at[way, k, s], d, next_f[way])
                todo.append((block, k, way))
        for block, k, way in todo:
            send(block, block, ag_leave[way], ag_sem.at[2 + way, k, s], d, near_f[way])

    block = hg_ref.at[f]
    for kind, reach in ((0, 2), (2, 1)):
        for k, y in ((0, yh), (1, 1 - yh)):
            for way in range(2):
                to = y * n_z + (z + (reach, -reach)[way] + n_z) % n_z
                send(block, block, ag_leave[way], ag_sem.at[kind + way, k, 0], d, to)
    send(block, block, agy_s, agy_r, d, f_y)

    mid_sum = jnp.sum(mg.astype(F32), axis=0, keepdims=True)
    hid_sum = jnp.sum(hg.astype(F32), axis=0, keepdims=True)
    gmt_ref[pl.ds(0, units), :] = lax.dot_general(
        act, mg, (((0,), (0,)), ((), ())), preferred_element_type=F32).astype(BF16)
    extra = gmt_ref.shape[0] - units
    at = lax.broadcasted_iota(jnp.int32, (extra, units), 0)
    tail = jnp.where(at == 0, mid_sum, jnp.where(at == 1, out_sum, jnp.where(at == 2, hid_sum, 0.0)))
    gmt_ref[pl.ds(units, extra), :] = tail.astype(BF16)
    gm_rows = gmr_ref.shape[1]

    def gm_scatter(o, _):
        to = (d + o) % n_dp

        @pl.when(to < act_ranks)
        def _():
            send(gmt_ref.at[rows(to, gm_rows)], gmr_ref.at[d], gm_s, gm_r, to, f)
        return 0

    lax.fori_loop(1, n_dp, gm_scatter, 0)

    def add_up(ref):
        acc = ref[0].astype(F32)
        for i in range(1, ref.shape[0]):
            acc = acc + ref[i].astype(F32)
        return acc.astype(BF16)

    n_b = z1_ref.shape[0]
    n_a = z2_ref.shape[0]
    za, zb = z // n_b, z % n_b

    def owners_only(task):
        pl.when(d < act_ranks)(task)

    half_rows = gm_rows // 2

    def gm_first():
        gmr_ref[d] = gmt_ref[rows(d, gm_rows), :]
        drain(gmr_ref.at[pl.ds(0, n_dp - 1)], gm_r)
        acc = gmr_ref[0].astype(F32)
        for i in range(1, n_dp):
            acc = acc + gmr_ref[i].astype(F32)
        low, high = acc[:half_rows], acc[half_rows:]
        yown_ref[...] = jnp.where(yh == 0, low, high)
        y2_ref[0] = jnp.where(yh == 0, high, low).astype(BF16)
        send(y2_ref.at[0], y2_ref.at[1], y2_s, y2_r, d, f_y)

    def gm_second():
        drain(y2_ref.at[1], y2_r)
        z1_ref[zb] = (yown_ref[...] + y2_ref[1].astype(F32)).astype(BF16)
        for o in range(1, n_b):
            to = yh * n_z + za * n_b + (zb + o) % n_b
            send(z1_ref.at[zb], z1_ref.at[zb], z1_s, z1_r, d, to)

    def gm_third():
        drain(z1_ref.at[pl.ds(0, n_b - 1)], z1_r)
        z2_ref[za] = add_up(z1_ref)
        for o in range(1, n_a):
            to = yh * n_z + ((za + o) % n_a) * n_b + zb
            send(z2_ref.at[za], z2_ref.at[za], z2_s, z2_r, d, to)

    def gm_fourth():
        if n_a > 1:
            drain(z2_ref.at[pl.ds(0, n_a - 1)], z2_r)
        block = gmf_ref.at[yh, rows(d, half_rows)]
        gmf_ref[yh, rows(d, half_rows), :] = add_up(z2_ref)

        def gm_spread(o, _):
            send(block, block, gmg_s, gmg_r, (d + o) % n_dp, f)
            return 0

        lax.fori_loop(1, n_dp, gm_spread, 0)

    def gm_pair():
        @pl.when(d < act_ranks)
        def _():
            drain(gmf_ref.at[0, pl.ds(0, half_rows * (act_ranks - 1))], gmg_r)

        @pl.when(d >= act_ranks)
        def _():
            drain(gmf_ref.at[0], gmg_r)

        send(gmf_ref.at[yh], gmf_ref.at[yh], gmy_s, gmy_r, d, f_y)

    for s in range(1, steps):
        ag_step(s)
        owners_only([gm_first, gm_second, gm_third][s - 1])
    drain(hg_ref.at[f_y], agy_r)
    for k in range(2):
        base = (yh if k == 0 else 1 - yh) * n_z
        drain(hg_ref.at[base + (z + n_z - far) % n_z], ag_sem.at[0, k, steps - 1])
        for s in range(steps):
            drain(hg_ref.at[base + (z + n_z - 1 - 2 * s) % n_z], ag_sem.at[2, k, s])
            drain(hg_ref.at[base + (z + 1 + 2 * s) % n_z], ag_sem.at[3, k, s])
    hg_all = hg_ref[...].reshape(n_ex, units)
    gpt_ref[...] = jnp.dot(feat_ref[...], hg_all, preferred_element_type=F32).astype(BF16)
    gp_rows = gpr_ref.shape[1]

    def gp_scatter(o, _):
        to = (d + o) % n_dp
        send(gpt_ref.at[rows(to, gp_rows)], gpr_ref.at[d], gp_s, gp_r, to, f)
        return 0

    lax.fori_loop(1, n_dp, gp_scatter, 0)
    gpr_ref[d] = gpt_ref[rows(d, gp_rows), :]

    drain(slot_ref.at[pl.ds(0, dim * (n_f - per))], wg_r)

    def place(r, _):
        for k, (oy, oz) in enumerate(offsets(r)):
            wt_ref[rows(field(oy, -oz), dim), :] = slot_ref[rows(r * per + k, dim), :]
        return 0

    lax.fori_loop(0, n_dp, place, 0)
    nt = (((1,), (1,)), ((), ()))
    blocks = 4

    def vg_block(i):
        size = v_ref.shape[0] // blocks
        at = pl.ds(i * size, size)
        both = lax.dot_general(w_ref[at, :], hg_all, nt, preferred_element_type=F32)
        both = both + lax.dot_general(wt_ref[at, :], hg_all, nt, preferred_element_type=F32)
        vg_ref[at, :] = (both * p_ref[at, :].astype(F32)).astype(BF16)

    for i in range(blocks // 2):
        vg_block(i)
        if i == 0:
            owners_only(gm_fourth)

    drain(gpr_ref.at[pl.ds(0, n_dp - 1)], gp_r)
    gpf_ref[rows(d, gp_rows), :] = add_up(gpr_ref)

    def gp_spread(o, _):
        block = gpf_ref.at[rows(d, gp_rows)]
        send(block, block, gpg_s, gpg_r, (d + o) % n_dp, f)
        return 0

    lax.fori_loop(1, n_dp, gp_spread, 0)

    for i in range(blocks // 2, blocks):
        vg_block(i)
    gm_pair()

    drain(gpf_ref.at[pl.ds(0, gp_rows * (n_dp - 1))], gpg_r)
    gp_ref[...] = gpf_ref[...].astype(F32)

    drain(gmf_ref.at[1 - yh], gmy_r)
    for y in range(2):
        gm_ref[:, y] = gmf_ref[y].reshape(act_ranks, half_rows, units).astype(F32)

    drain(v_ref.at[pl.ds(0, dim * (n_f - 1))], a2a_s)


    @pl.when(d == 0)
    def _():
        drain(slot_ref.at[pl.ds(0, dim * (per - 1))], w_s)

    @pl.when(d != 0)
    def _():
        drain(slot_ref.at[pl.ds(0, dim * per)], w_s)

    drain(slot_ref.at[pl.ds(0, dim * per * (n_dp - 1))], wg_s)
    drain(partb_ref.at[pl.ds(0, 2 * far)], up_s)
    drain(partb_ref.at[pl.ds(0, 2 * (far - 1))], dn_s)
    drain(yx_ref, yx_s)
    drain(hg_ref.at[0], agy_s)
    drain(hg_ref.at[pl.ds(0, 2 * far)], agu_s)
    drain(hg_ref.at[pl.ds(0, 2 * (far - 1))], agd_s)

    @pl.when(d < act_ranks)
    def _():
        drain(gmt_ref.at[pl.ds(0, gm_rows * (act_ranks - 1))], gm_s)
        drain(z1_ref.at[pl.ds(0, n_b - 1)], z1_s)
        if n_a > 1:
            drain(z2_ref.at[pl.ds(0, n_a - 1)], z2_s)
        drain(y2_ref.at[0], y2_s)
        drain(slot_ref.at[pl.ds(0, half_rows * (n_dp - 1))], gmg_s)

    @pl.when(d >= act_ranks)
    def _():
        drain(gmt_ref.at[pl.ds(0, gm_rows * act_ranks)], gm_s)

    drain(gmf_ref.at[0], gmy_s)
    drain(gpt_ref.at[pl.ds(0, gp_rows * (n_dp - 1))], gp_s)
    drain(gpf_ref.at[pl.ds(0, gp_rows * (n_dp - 1))], gpg_s)


def per_device(n_dp, n_f, vectors, labels, pair_weight, hidden_bias, mid_weight, mid_bias, out_weight):
    n_ex, _, _, dim = vectors.shape
    units = pair_weight.shape[3]
    feats = n_f * dim
    share = n_ex // n_f
    n_z = n_f // 2
    steps = n_z // 4
    gp_rows = feats // n_dp
    gm_rows = 16 * -(-(units + 3) // (16 * n_dp))
    act_ranks = -(-(units + 3) // gm_rows)
    n_b = min(4, n_z)
    n_a = n_z // n_b
    v = jnp.transpose(vectors, (1, 2, 3, 0)).reshape(feats, n_ex)
    vmem = pl.BlockSpec(memory_space=pltpu.VMEM)
    dma = pltpu.SemaphoreType.DMA
    vg, gp, gm = pl.pallas_call(
        functools.partial(kernel, n_dp, n_f, dim, act_ranks),
        out_shape=(
            jax.ShapeDtypeStruct((feats, n_ex), BF16),
            jax.ShapeDtypeStruct((feats, units), F32),
            jax.ShapeDtypeStruct((act_ranks, 2, gm_rows // 2, units), F32),
        ),
        in_specs=[vmem] * 7,
        out_specs=(vmem,) * 3,
        scratch_shapes=[
            pltpu.VMEM((feats, units), BF16),
            pltpu.VMEM((feats, n_ex), BF16),
            pltpu.VMEM((feats, n_ex), BF16),
            pltpu.VMEM((feats, units), BF16),
            pltpu.VMEM((n_f, share, units), F32),
            pltpu.VMEM((n_f, share, units), BF16),
            pltpu.VMEM((2, 2, steps, share, units), BF16),
            pltpu.VMEM((2, 2, steps, share, units), BF16),
            pltpu.VMEM((share, units), BF16),
            pltpu.VMEM((n_f, share, units), BF16),
            pltpu.VMEM((gm_rows * act_ranks, units), BF16),
            pltpu.VMEM((n_dp, gm_rows, units), BF16),
            pltpu.VMEM((gm_rows // 2, units), F32),
            pltpu.VMEM((2, gm_rows // 2, units), BF16),
            pltpu.VMEM((n_b, gm_rows // 2, units), BF16),
            pltpu.VMEM((n_a, gm_rows // 2, units), BF16),
            pltpu.VMEM((2, gm_rows // 2 * act_ranks, units), BF16),
            pltpu.VMEM((feats, units), BF16),
            pltpu.VMEM((n_dp, gp_rows, units), BF16),
            pltpu.VMEM((feats, units), BF16),
            dma((30,)),
            dma((4, 2, steps)),
            dma((4, 2, steps)),
        ],
        compiler_params=pltpu.CompilerParams(
            collective_id=0, has_side_effects=True, vmem_limit_bytes=48 * 1024 * 1024
        ),
        name="train_step",
    )(
        v,
        labels.reshape(n_ex // 128, 128),
        pair_weight.reshape(feats, units),
        hidden_bias.reshape(1, units),
        mid_weight,
        mid_bias.reshape(1, units),
        out_weight.reshape(1, units),
    )
    gm = gm.reshape(act_ranks * gm_rows, units)
    vector_grad = jnp.transpose(vg.reshape(1, n_f, dim, n_ex), (3, 0, 1, 2))
    return (
        vector_grad,
        gp.reshape(1, n_f, dim, units),
        gm[units + 2],
        gm[:units],
        gm[units],
        gm[units + 1],
    )


def solution(mesh):
    in_specs = (
        P("dp", "field", None, None),
        P("dp"),
        P("field", None, None, None),
        P(),
        P(),
        P(),
        P(),
    )
    out_specs = (P("dp", "field", None, None), P("field", None, None, None), P(), P(), P(), P())
    body = functools.partial(per_device, mesh.shape["dp"], mesh.shape["field"])
    return jax.shard_map(body, mesh=mesh, in_specs=in_specs, out_specs=out_specs, check_vma=False)
```
